256 devices in a mesh: blk: 16 (over x, y_lo, core), en: 16 (over y_hi, z).
Axes of the slice: x: 4, y: 4 (y_hi: 2, y_lo: 2; y = y_hi * 2 + y_lo), z: 8, core: 2. Of those that a mesh axis runs over, the one named last changes fastest.
Arguments:
- panel: bfloat16 [64, 8192, 1024], P('en', 'blk'), may hold values from -0.26367188 to 0.26367188
- gamma: bfloat16 [64, 2, 512, 512], P('en'), may hold values from -1 to 3, as said below
- energy_point: int32 [64], P('en'), may hold values from 0 to 63, each once
Outputs:
- density: float32 [8192, 4, 512], P(('blk', 'en'))
The draws below stay inside these ranges and needn't reach their ends.
Inputs may be any that keep to these rules, and one draw needn't show every extreme that they name: For each energy, gamma holds the real part (symmetric) and the imaginary part (antisymmetric) of a Hermitian matrix. `energy_point`: each grid point appears once.
All inputs are finite; a program needn't handle non-finite values.
Results may differ from the reference program's by a relative error of at most 0.00053.
Values may be sent and summed in bfloat16 or wider, within the bound.
A program may use at most 128 MiB of HBM per device.

```python
import jax
import jax.numpy as jnp
import numpy as np
from jax import lax

C = 512
BLK_ROWS = 512
ROUNDS = 3
SLOTS = 4
NORB = 8192
ENERGIES = 64
N_BLK = 16


def draw_gamma(key, part):
    key = jax.random.fold_in(key, 11)
    key_diag, key_real, key_imag = jax.random.split(key, 3)
    diag_values = jnp.exp(jax.random.uniform(key_diag, (ENERGIES, C), jnp.float32, jnp.log(1.5), jnp.log(3.0)))
    spread = C ** (-0.5)
    real_noise = jax.random.uniform(key_real, (ENERGIES, C, C), jnp.float32, -1.0, 1.0) * spread
    imag_noise = jax.random.uniform(key_imag, (ENERGIES, C, C), jnp.float32, -1.0, 1.0) * spread
    identity = (jnp.arange(C)[:, None] == jnp.arange(C)[None, :]).astype(jnp.float32)
    off_mask = 1.0 - identity
    real_part = 0.5 * (real_noise + jnp.swapaxes(real_noise, 1, 2)) * off_mask + identity[None] * diag_values[:, :, None]
    imaginary_piece = 0.5 * (imag_noise - jnp.swapaxes(imag_noise, 1, 2))
    return jnp.stack([real_part, imaginary_piece], axis=1).astype(jnp.bfloat16)


def block_scale(key, shape, cuts, smallest, largest):
    level, own = 1.0, jax.random.fold_in(key, 6)
    for axis_at, shards_of in cuts:
        steps = jnp.exp(jax.random.uniform(jax.random.fold_in(own, axis_at), (shards_of,), jnp.float32, smallest / len(cuts), largest / len(cuts)))
        level = level * jnp.repeat(steps, shape[axis_at] // shards_of).reshape([-1 if axis == axis_at else 1 for axis in range(len(shape))])
    return level


def centred(key, extent, scale, most, cuts=(), held_as=jnp.bfloat16):
    values = scale * jax.random.normal(key, extent, jnp.float32)
    if cuts:
        values = values * block_scale(key, extent, cuts, -0.22, 0.18)
    return jnp.clip(values, -most, most).astype(held_as)


def setup_inputs(seed: int = 0) -> dict:
    arg_keys = jax.random.split(jax.random.key(seed), 4)
    panel = centred(arg_keys[0], (ENERGIES, NORB, 2 * C), (C ** -0.5), 0.26367188, ((0, 16), (1, 16)))
    gamma = draw_gamma(jax.random.fold_in(arg_keys[3], 71), 0)
    energy_point = jax.random.permutation(arg_keys[2], ENERGIES).astype(jnp.int32)
    return {"panel": panel, "gamma": gamma, "energy_point": energy_point}


THERMAL_LEVEL = 0.1


def window_weight(energy_point, energies):
    energy_grid = (energy_point.astype(jnp.float32) + 0.5) / energies - 0.5
    upper_block = jax.nn.sigmoid((0.5 - energy_grid) / THERMAL_LEVEL)
    lower_block = jax.nn.sigmoid((-0.5 - energy_grid) / THERMAL_LEVEL)
    return (upper_block - lower_block) / energies


def block_form(gamma_one):
    real_part = gamma_one[0]
    imaginary_piece = gamma_one[1]
    upper_rows = jnp.concatenate([real_part, imaginary_piece], axis=1)
    lower_rows = jnp.concatenate([-imaginary_piece, real_part], axis=1)
    return jnp.concatenate([upper_rows, lower_rows], axis=0)


def reference(panel, gamma, energy_point):
    weights = window_weight(energy_point, ENERGIES)
    orders = [np.arange(N_BLK) ^ 0] + [np.arange(N_BLK) ^ (1 << level) for level in range(ROUNDS)]

    def one_energy(total, inputs):
        grid_panel, gamma_one, fermi_weight = inputs
        mixed = (fermi_weight * jnp.dot(grid_panel, block_form(gamma_one), preferred_element_type=jnp.float32)).astype(jnp.bfloat16)
        mixed_blocks = mixed.reshape(N_BLK, BLK_ROWS, 2 * C).astype(jnp.float32)
        panel_blocks = grid_panel.reshape(N_BLK, BLK_ROWS, 2 * C).astype(jnp.float32)
        slot_term_list = [jnp.einsum("ira,ica->irc", mixed_blocks, panel_blocks[order]) for order in orders]
        term = jnp.stack(slot_term_list, axis=2).reshape(NORB, SLOTS, BLK_ROWS)
        return total + term, None

    total = jnp.zeros((NORB, SLOTS, BLK_ROWS), jnp.float32)
    total, unused = lax.scan(one_energy, total, (panel, gamma, weights))
    return total
```

```python
import functools

import jax
import jax.numpy as jnp
from jax import lax
from jax.experimental import pallas as pl
from jax.experimental.pallas import tpu as pltpu
from jax.sharding import PartitionSpec as P

THERMAL_LEVEL = 0.1
ENERGIES = 64
Z = 8
MESH = pl.DeviceIdType.MESH
F32 = jnp.float32
BF16 = jnp.bfloat16


def window_weight(energy_point, shape):
    grid = (jnp.full(shape, energy_point.astype(F32)) + 0.5) / ENERGIES - 0.5
    upper = jax.nn.sigmoid((0.5 - grid) / THERMAL_LEVEL)
    lower = jax.nn.sigmoid((-0.5 - grid) / THERMAL_LEVEL)
    return (upper - lower) / ENERGIES


def dot(a, b):
    return jnp.dot(a, b, preferred_element_type=F32)


def dot_nt(a, b):
    return lax.dot_general(a, b, (((1,), (1,)), ((), ())), preferred_element_type=F32)


def interleave(first, second):
    group = lax.broadcasted_iota(jnp.int32, (32, 128), 1) // 16
    halves = []
    for low in (0, 4):
        total = jnp.zeros((32, 128), F32)
        for at in range(8):
            source = first if at % 2 == 0 else second
            shift = (16 * (at - at // 2 - low)) % 128
            moved = pltpu.roll(source, shift, 1) if shift else source
            total = jnp.where(group == at, moved, total)
        halves.append(total)
    return jnp.concatenate(halves, axis=1)


def kernel(energy, panel, panel_rows, gamma, out,
           own, near, far, broad, mixed, part, ring, give, got, q_part, q_got, t_part, t_got,
           own_sem, broad_sem, near_sem, far_send, far_recv, ring_send, ring_recv,
           give_sem, q_send, q_recv, t_send, t_recv):
    b, k = lax.axis_index("blk"), lax.axis_index("en")
    core, y_lo, x_lo = b % 2, (b // 2) % 2, (b // 4) % 2
    y_hi, z = k // Z, k % Z
    parity = (core + y_lo + x_lo) % 2
    core_mate = b + 1 - 2 * core
    y_mate = b + 2 - 4 * y_lo
    x_mate = b + 4 - 8 * x_lo
    to = parity * x_mate + (1 - parity) * y_mate
    source = parity * y_mate + (1 - parity) * x_mate
    k_mate = k + Z - 2 * Z * y_hi
    sign = 1 - 2 * core
    ahead = y_hi * Z + (z + sign + Z) % Z
    behind = y_hi * Z + (z - sign + Z) % Z

    loads = []
    for e in range(4):
        loads.append((pltpu.make_async_copy(panel.at[e], own.at[e], own_sem.at[e]),
                      pltpu.make_async_copy(gamma.at[e], broad.at[e], broad_sem.at[e])))
        for load in loads[-1]:
            load.start()

    barrier = pltpu.get_barrier_semaphore()
    peers = [(b, ahead), (b, behind), (core_mate, k), (y_mate, k), (x_mate, k),
             (b, k_mate), (y_mate, k_mate), (x_mate, k_mate)]
    for peer in peers:
        pl.semaphore_signal(barrier, inc=1, device_id=peer, device_id_type=MESH)
    pl.semaphore_wait(barrier, len(peers))

    def remote(src, dst, send, recv, device):
        return pltpu.make_async_remote_copy(src_ref=src, dst_ref=dst, send_sem=send, recv_sem=recv,
                                            device_id=device, device_id_type=MESH)

    sent = []

    def send(copy):
        copy.start()
        sent.append(copy)

    far_copies = [remote(panel_rows.at[:, c // 2, :, c % 2], far.at[c], far_send.at[c], far_recv.at[c], (to, k))
                  for c in range(4)]
    for copy in far_copies:
        send(copy)
    near_copy = remote(panel, near, near_sem.at[0], near_sem.at[1], (core_mate, k))
    send(near_copy)

    for e in range(4):
        for load in loads[e]:
            load.wait()
        weight = window_weight(energy[e], (1, 256))

        def columns(n, carry, e=e, weight=weight):
            at = pl.ds(pl.multiple_of(n * 256, 256), 256)
            real, imaginary = own[e, :, :512], own[e, :, 512:]
            gamma_real, gamma_imaginary = broad[e, 0, :, at], broad[e, 1, :, at]
            mixed[e, :, at] = (weight * (dot(real, gamma_real) - dot(imaginary, gamma_imaginary))).astype(BF16)
            mixed[e, :, pl.ds(pl.multiple_of(512 + n * 256, 256), 256)] = (
                weight * (dot(real, gamma_imaginary) + dot(imaginary, gamma_real))).astype(BF16)
            return carry

        lax.fori_loop(0, 2, columns, 0)

    def ring_copy(u, step):
        first = step in (0, 4)
        if step < 4:
            device, src = (b, ahead), part.at[u, (z + 4 * sign + Z) % Z] if first else ring.at[u, step - 1]
        else:
            device, src = (b, behind), part.at[u, (z - 3 * sign + Z) % Z] if first else ring.at[u, step - 1]
        return remote(src, ring.at[u, step], ring_send.at[u, step], ring_recv.at[u, step], device)

    def ring_first(u):
        send(ring_copy(u, 0))
        send(ring_copy(u, 4))

    def ring_next(u, step):
        ring_copy(u, step - 1).wait_recv()
        ring[u, step - 1] += part[u, (z + (4 - step) * sign + Z) % Z]
        send(ring_copy(u, step))
        if step < 3:
            ring_copy(u, step + 3).wait_recv()
            ring[u, step + 3] += part[u, (z - (3 - step) * sign + Z) % Z]
            send(ring_copy(u, step + 4))

    def ring_wait(u):
        ring_copy(u, 3).wait_recv()
        ring_copy(u, 6).wait_recv()

    def ring_total(u):
        return part[u, z] + ring[u, 3] + ring[u, 6]

    def whole_block(slot, rows):
        def columns(n, carry):
            at = pl.ds(pl.multiple_of(n * 256, 256), 256)
            total = dot_nt(mixed[0], rows[0, at, :])
            for e in range(1, 4):
                total += dot_nt(mixed[e], rows[e, at, :])
            part[2 * slot, :, :, at] = total[:256].reshape(8, 32, 256)
            part[2 * slot + 1, :, :, at] = total[256:].reshape(8, 32, 256)
            return carry

        lax.fori_loop(0, 2, columns, 0)
        ring_first(2 * slot)
        ring_first(2 * slot + 1)

    def give_copy(slot):
        return remote(give.at[slot], got.at[slot], give_sem.at[slot, 0], give_sem.at[slot, 1], (b, k_mate))

    def whole_end(slot):
        ring_wait(2 * slot)
        ring_wait(2 * slot + 1)
        give[slot] = ring_total(2 * slot + 1 - y_hi)
        send(give_copy(slot))
        out[slot] = ring_total(2 * slot + y_hi)

    def chunk_block(c):
        far_copies[c].wait_recv()

        def columns(n, carry):
            at = pl.ds(pl.multiple_of(n * 256, 256), 256)
            total = dot_nt(far[c, 0].reshape(128, 1024), mixed[0, at, :])
            for e in range(1, 4):
                total += dot_nt(far[c, e].reshape(128, 1024), mixed[e, at, :])
            part[4 + c, :, 0:16, at] = total.reshape(8, 16, 256)
            turned = total.T.reshape(8, 2, 16, 128)
            for low in range(2):
                part[4 + c, :, 16:32, pl.ds(pl.multiple_of(n * 256 + low * 128, 128), 128)] = turned[:, low]
            return carry

        lax.fori_loop(0, 2, columns, 0)
        ring_first(4 + c)

    def q_copy(c):
        return remote(q_part.at[c, 1 - y_hi], q_got.at[c], q_send.at[c], q_recv.at[c], (b, k_mate))

    def t_copy(c, from_y):
        return remote(t_part.at[c], t_got.at[c % 2, from_y], t_send.at[c], t_recv.at[c % 2, from_y],
                      (source, (c // 2) * Z + z))

    def chunk_end(c):
        ring_wait(4 + c)
        total = ring_total(4 + c)
        t_part[c] = total[:16]
        send(t_copy(c, y_hi))
        q_part[c, 0] = total[16:, :256]
        q_part[c, 1] = total[16:, 256:]
        send(q_copy(c))

    whole_block(0, own)
    near_copy.wait_recv()
    whole_block(1, near)
    for u in range(4):
        ring_next(u, 1)
    chunk_block(0)
    for u in range(4):
        ring_next(u, 2)
    ring_next(4, 1)
    for u in range(4):
        ring_next(u, 3)
    ring_next(4, 2)
    whole_end(0)
    whole_end(1)
    ring_next(4, 3)
    chunk_block(1)
    chunk_end(0)
    for step in (1, 2, 3):
        ring_next(5, step)
    chunk_end(1)
    chunk_block(2)
    for step in (1, 2, 3):
        ring_next(6, step)
    chunk_end(2)
    chunk_block(3)
    for step in (1, 2, 3):
        ring_next(7, step)
    chunk_end(3)

    for slot in range(2):
        give_copy(slot).wait_recv()
        out[slot] += got[slot]
    for c in range(4):
        q_copy(c).wait_recv()
    for h in range(2):
        pieces = []
        for c in (2 * h, 2 * h + 1):
            total = q_part[c, y_hi] + q_got[c]
            pieces.append(jnp.concatenate([total[:, :128], total[:, 128:]], axis=0))
        out[3 - parity, :, 256 * h:256 * h + 256] = interleave(*pieces)
    for half in range(2):
        for from_y in range(2):
            t_copy(half, from_y).wait_recv()
        out[2 + parity, 16 * half:16 * half + 16] = t_got[half, 0] + t_got[half, 1]
    for copy in sent:
        copy.wait_send()


def local(panel, gamma, energy_point):
    any_space = pl.BlockSpec(memory_space=pl.ANY)
    dma = pltpu.SemaphoreType.DMA
    blocks = pl.pallas_call(
        kernel,
        out_shape=jax.ShapeDtypeStruct((4, 32, 512), F32),
        in_specs=[pl.BlockSpec(memory_space=pltpu.SMEM), any_space, any_space, any_space],
        out_specs=pl.BlockSpec(memory_space=pltpu.VMEM),
        scratch_shapes=[
            pltpu.VMEM((4, 512, 1024), BF16),
            pltpu.VMEM((4, 512, 1024), BF16),
            pltpu.VMEM((4, 4, 8, 16, 1024), BF16),
            pltpu.VMEM((4, 2, 512, 512), BF16),
            pltpu.VMEM((4, 512, 1024), BF16),
            pltpu.VMEM((8, 8, 32, 512), F32),
            pltpu.VMEM((8, 7, 32, 512), F32),
            pltpu.VMEM((2, 32, 512), F32),
            pltpu.VMEM((2, 32, 512), F32),
            pltpu.VMEM((4, 2, 16, 256), F32),
            pltpu.VMEM((4, 16, 256), F32),
            pltpu.VMEM((4, 16, 512), F32),
            pltpu.VMEM((2, 2, 16, 512), F32),
            dma((4,)), dma((4,)), dma((2,)), dma((4,)), dma((4,)), dma((8, 7)), dma((8, 7)),
            dma((2, 2)), dma((4,)), dma((4,)), dma((4,)), dma((2, 2)),
        ],
        compiler_params=pltpu.CompilerParams(collective_id=0, has_side_effects=True, vmem_limit_bytes=56 * 2**20),
        cost_estimate=pl.CostEstimate(flops=13_000_000_000, bytes_accessed=12 * 2**20, transcendentals=0),
        name="density",
    )(energy_point, panel, panel.reshape(4, 2, 8, 2, 16, 1024), gamma)
    return jnp.transpose(blocks, (1, 0, 2))


def solution(mesh):
    in_specs = (P("en", "blk", None), P("en", None, None, None), P("en"))
    out_specs = P(("blk", "en"), None, None)
    return jax.shard_map(local, mesh=mesh, in_specs=in_specs, out_specs=out_specs, check_vma=False)
```

```python
import functools

import jax
import jax.numpy as jnp
from jax import lax
from jax.experimental import pallas as pl
from jax.experimental.pallas import tpu as pltpu
from jax.sharding import PartitionSpec as P

THERMAL_LEVEL = 0.1
ENERGIES = 64
Z = 8
MESH = pl.DeviceIdType.MESH
F32 = jnp.float32
BF16 = jnp.bfloat16


def window_weight(energy_point, shape):
    grid = (jnp.full(shape, energy_point.astype(F32)) + 0.5) / ENERGIES - 0.5
    upper = jax.nn.sigmoid((0.5 - grid) / THERMAL_LEVEL)
    lower = jax.nn.sigmoid((-0.5 - grid) / THERMAL_LEVEL)
    return (upper - lower) / ENERGIES


def dot(a, b):
    return jnp.dot(a, b, preferred_element_type=F32)


def dot_nt(a, b):
    return lax.dot_general(a, b, (((1,), (1,)), ((), ())), preferred_element_type=F32)


def interleave(first, second):
    group = lax.broadcasted_iota(jnp.int32, (32, 128), 1) // 16
    halves = []
    for low in (0, 4):
        total = jnp.zeros((32, 128), F32)
        for at in range(8):
            source = first if at % 2 == 0 else second
            shift = (16 * (at - at // 2 - low)) % 128
            moved = pltpu.roll(source, shift, 1) if shift else source
            total = jnp.where(group == at, moved, total)
        halves.append(total)
    return jnp.concatenate(halves, axis=1)


def kernel(energy, panel, panel_rows, gamma, out,
           own, near, far, broad, mixed, part, ring, piece, piece_got, give, got, q_part, q_got, t_part, t_got,
           own_sem, broad_sem, near_sem, far_send, far_recv, ring_send, ring_recv, piece_send, piece_recv,
           give_sem, q_send, q_recv, t_send, t_recv):
    b, k = lax.axis_index("blk"), lax.axis_index("en")
    core, y_lo, x_lo = b % 2, (b // 2) % 2, (b // 4) % 2
    y_hi, z = k // Z, k % Z
    parity = (core + y_lo + x_lo) % 2
    core_mate = b + 1 - 2 * core
    y_mate = b + 2 - 4 * y_lo
    x_mate = b + 4 - 8 * x_lo
    to = parity * x_mate + (1 - parity) * y_mate
    source = parity * y_mate + (1 - parity) * x_mate
    k_mate = k + Z - 2 * Z * y_hi
    sign = 1 - 2 * core
    ahead = y_hi * Z + (z + sign + Z) % Z
    behind = y_hi * Z + (z - sign + Z) % Z

    loads = []
    for e in range(4):
        loads.append((pltpu.make_async_copy(panel.at[e], own.at[e], own_sem.at[e]),
                      pltpu.make_async_copy(gamma.at[e], broad.at[e], broad_sem.at[e])))
        for load in loads[-1]:
            load.start()

    barrier = pltpu.get_barrier_semaphore()
    peers = [(b, y_hi * Z + (z + d) % Z) for d in range(1, Z)] + [
        (core_mate, k), (y_mate, k), (x_mate, k),
        (b, k_mate), (y_mate, k_mate), (x_mate, k_mate)]
    for peer in peers:
        pl.semaphore_signal(barrier, inc=1, device_id=peer, device_id_type=MESH)
    pl.semaphore_wait(barrier, len(peers))

    def remote(src, dst, send, recv, device):
        return pltpu.make_async_remote_copy(src_ref=src, dst_ref=dst, send_sem=send, recv_sem=recv,
                                            device_id=device, device_id_type=MESH)

    sent = []

    def send(copy):
        copy.start()
        sent.append(copy)

    far_copies = [remote(panel_rows.at[:, c // 2, :, c % 2], far.at[c], far_send.at[c], far_recv.at[c], (to, k))
                  for c in range(4)]
    for copy in far_copies:
        send(copy)
    near_copy = remote(panel, near, near_sem.at[0], near_sem.at[1], (core_mate, k))
    send(near_copy)

    for e in range(4):
        for load in loads[e]:
            load.wait()
        weight = window_weight(energy[e], (1, 256))

        def columns(n, carry, e=e, weight=weight):
            at = pl.ds(pl.multiple_of(n * 256, 256), 256)
            real, imaginary = own[e, :, :512], own[e, :, 512:]
            gamma_real, gamma_imaginary = broad[e, 0, :, at], broad[e, 1, :, at]
            mixed[e, :, at] = (weight * (dot(real, gamma_real) - dot(imaginary, gamma_imaginary))).astype(BF16)
            mixed[e, :, pl.ds(pl.multiple_of(512 + n * 256, 256), 256)] = (
                weight * (dot(real, gamma_imaginary) + dot(imaginary, gamma_real))).astype(BF16)
            return carry

        lax.fori_loop(0, 2, columns, 0)

    def ring_copy(u, step):
        first = step in (0, 4)
        if step < 4:
            device, src = (b, ahead), part.at[u, (z + 4 * sign + Z) % Z] if first else ring.at[u, step - 1]
        else:
            device, src = (b, behind), part.at[u, (z - 3 * sign + Z) % Z] if first else ring.at[u, step - 1]
        return remote(src, ring.at[u, step], ring_send.at[u, step], ring_recv.at[u, step], device)

    def ring_first(u):
        send(ring_copy(u, 0))
        send(ring_copy(u, 4))

    def ring_next(u, step):
        ring_copy(u, step - 1).wait_recv()
        ring[u, step - 1] += part[u, (z + (4 - step) * sign + Z) % Z]
        send(ring_copy(u, step))
        if step < 3:
            ring_copy(u, step + 3).wait_recv()
            ring[u, step + 3] += part[u, (z - (3 - step) * sign + Z) % Z]
            send(ring_copy(u, step + 4))

    def ring_wait(u):
        ring_copy(u, 3).wait_recv()
        ring_copy(u, 6).wait_recv()

    def ring_total(u):
        return part[u, z] + ring[u, 3] + ring[u, 6]

    def whole_block(slot, rows):
        def columns(n, carry):
            at = pl.ds(pl.multiple_of(n * 256, 256), 256)
            total = dot_nt(mixed[0], rows[0, at, :])
            for e in range(1, 4):
                total += dot_nt(mixed[e], rows[e, at, :])
            part[2 * slot, :, :, at] = total[:256].reshape(8, 32, 256)
            part[2 * slot + 1, :, :, at] = total[256:].reshape(8, 32, 256)
            return carry

        lax.fori_loop(0, 2, columns, 0)
        ring_first(2 * slot)
        ring_first(2 * slot + 1)

    def give_copy(slot):
        return remote(give.at[slot], got.at[slot], give_sem.at[slot, 0], give_sem.at[slot, 1], (b, k_mate))

    def whole_end(slot):
        ring_wait(2 * slot)
        ring_wait(2 * slot + 1)
        give[slot] = ring_total(2 * slot + 1 - y_hi)
        send(give_copy(slot))
        out[slot] = ring_total(2 * slot + y_hi)

    def piece_copy(c, d):
        return remote(piece.at[c, (z + d) % Z], piece_got.at[c, d - 1], piece_send.at[c, d - 1], piece_recv.at[c, d - 1],
                      (b, y_hi * Z + (z + d) % Z))

    def chunk_block(c):
        far_copies[c].wait_recv()

        def columns(n, carry):
            at = pl.ds(pl.multiple_of(n * 256, 256), 256)
            total = dot_nt(far[c, 0].reshape(128, 1024), mixed[0, at, :])
            for e in range(1, 4):
                total += dot_nt(far[c, e].reshape(128, 1024), mixed[e, at, :])
            rows = total.reshape(8, 16, 256)
            part[4 + c, :, 0:16, at] = rows
            piece[c, :, 0:16, at] = rows.astype(BF16)
            turned = total.T.reshape(8, 2, 16, 128)
            for low in range(2):
                lanes = pl.ds(pl.multiple_of(n * 256 + low * 128, 128), 128)
                part[4 + c, :, 16:32, lanes] = turned[:, low]
                piece[c, :, 16:32, lanes] = turned[:, low].astype(BF16)
            return carry

        lax.fori_loop(0, 2, columns, 0)
        for d in (4, 3, 5, 2, 6, 1, 7):
            send(piece_copy(c, d))

    def q_copy(c):
        return remote(q_part.at[c, 1 - y_hi], q_got.at[c], q_send.at[c], q_recv.at[c], (b, k_mate))

    def t_copy(c, from_y):
        return remote(t_part.at[c], t_got.at[c % 2, from_y], t_send.at[c], t_recv.at[c % 2, from_y],
                      (source, (c // 2) * Z + z))

    def chunk_end(c):
        total = part[4 + c, z]
        for d in (1, 7, 2, 6, 3, 5, 4):
            piece_copy(c, d).wait_recv()
            total += piece_got[c, d - 1].astype(F32)
        t_part[c] = total[:16]
        send(t_copy(c, y_hi))
        q_part[c, 0] = total[16:, :256]
        q_part[c, 1] = total[16:, 256:]
        send(q_copy(c))

    whole_block(0, own)
    near_copy.wait_recv()
    whole_block(1, near)
    chunk_block(0)
    for u in range(4):
        ring_next(u, 1)
    for u in range(4):
        ring_next(u, 2)
    chunk_block(1)
    for u in range(4):
        ring_next(u, 3)
    chunk_end(0)
    whole_end(0)
    whole_end(1)
    chunk_block(2)
    chunk_end(1)
    chunk_block(3)
    chunk_end(2)
    chunk_end(3)

    for slot in range(2):
        give_copy(slot).wait_recv()
        out[slot] += got[slot]
    for c in range(4):
        q_copy(c).wait_recv()
    for h in range(2):
        pieces = []
        for c in (2 * h, 2 * h + 1):
            total = q_part[c, y_hi] + q_got[c]
            pieces.append(jnp.concatenate([total[:, :128], total[:, 128:]], axis=0))
        out[3 - parity, :, 256 * h:256 * h + 256] = interleave(*pieces)
    for half in range(2):
        for from_y in range(2):
            t_copy(half, from_y).wait_recv()
        out[2 + parity, 16 * half:16 * half + 16] = t_got[half, 0] + t_got[half, 1]
    for copy in sent:
        copy.wait_send()


def local(panel, gamma, energy_point):
    any_space = pl.BlockSpec(memory_space=pl.ANY)
    dma = pltpu.SemaphoreType.DMA
    blocks = pl.pallas_call(
        kernel,
        out_shape=jax.ShapeDtypeStruct((4, 32, 512), F32),
        in_specs=[pl.BlockSpec(memory_space=pltpu.SMEM), any_space, any_space, any_space],
        out_specs=pl.BlockSpec(memory_space=pltpu.VMEM),
        scratch_shapes=[
            pltpu.VMEM((4, 512, 1024), BF16),
            pltpu.VMEM((4, 512, 1024), BF16),
            pltpu.VMEM((4, 4, 8, 16, 1024), BF16),
            pltpu.VMEM((4, 2, 512, 512), BF16),
            pltpu.VMEM((4, 512, 1024), BF16),
            pltpu.VMEM((8, 8, 32, 512), F32),
            pltpu.VMEM((4, 7, 32, 512), F32),
            pltpu.VMEM((4, 8, 32, 512), BF16),
            pltpu.VMEM((4, 7, 32, 512), BF16),
            pltpu.VMEM((2, 32, 512), F32),
            pltpu.VMEM((2, 32, 512), F32),
            pltpu.VMEM((4, 2, 16, 256), F32),
            pltpu.VMEM((4, 16, 256), F32),
            pltpu.VMEM((4, 16, 512), F32),
            pltpu.VMEM((2, 2, 16, 512), F32),
            dma((4,)), dma((4,)), dma((2,)), dma((4,)), dma((4,)), dma((4, 7)), dma((4, 7)), dma((4, 7)), dma((4, 7)),
            dma((2, 2)), dma((4,)), dma((4,)), dma((4,)), dma((2, 2)),
        ],
        compiler_params=pltpu.CompilerParams(collective_id=0, has_side_effects=True, vmem_limit_bytes=56 * 2**20),
        cost_estimate=pl.CostEstimate(flops=13_000_000_000, bytes_accessed=12 * 2**20, transcendentals=0),
        name="density",
    )(energy_point, panel, panel.reshape(4, 2, 8, 2, 16, 1024), gamma)
    return jnp.transpose(blocks, (1, 0, 2))


def solution(mesh):
    in_specs = (P("en", "blk", None), P("en", None, None, None), P("en"))
    out_specs = P(("blk", "en"), None, None)
    return jax.shard_map(local, mesh=mesh, in_specs=in_specs, out_specs=out_specs, check_vma=False)
```
